32 devices in a mesh: groups: 2 (over x), dp: 8 (over z, y), tensor: 2 (over core).
Axes of the slice: x: 2, y: 2, z: 4, core: 2. Of those that a mesh axis runs over, the one named last changes fastest.
Arguments:
- pre_act: bfloat16 [32, 256, 13824], P(('groups', 'dp'), None, 'tensor'), parts along dimension 0, may hold values from -6 to 6
- out_grad: bfloat16 [32, 256, 5120], P(('groups', 'dp'), None, 'tensor'), parts along dimension 0, may hold values from -6 to 6
- counts: int32 [32], P(('groups', 'dp')), parts along dimension 0, may hold values from 1 to 256
- proj_in: bfloat16 [13824, 64], P('tensor'), may hold values from -0.0546875 to 0.0546875
- proj_out: bfloat16 [5120, 64], P('tensor'), may hold values from -0.078125 to 0.078125
- query_grads: bfloat16 [512, 4096], P(('dp', 'tensor')), may hold values from -0.09375 to 0.09375
Outputs:
- scores: float32 [32, 512], P('groups', ('dp', 'tensor')), parts along dimension 0
The draws below stay inside these ranges and needn't reach their ends.
There are 2 independent parts, one for each index of `groups`. The reference program is written for one: setup_inputs(seed, part) draws one part's arguments, and reference() takes and returns one part's arrays. A program takes and returns all parts, laid end to end along the dimension named above; an argument that names none is the same for every part. Nothing has to cross between parts.
All inputs are finite; a program needn't handle non-finite values.
Results may differ from the reference program's by a relative error of at most 0.0042.
Values may be sent and summed in bfloat16 or wider, within the bound.
A program may use at most 64 MiB of HBM per device.

```python
import jax
import jax.numpy as jnp
from jax import lax

D = 5120
FF = 13824
SEQ = 256
RANK = 64
EXAMPLES = 16
QUERIES = 512


def with_ends(drawn, rng, smallest, high):
    place = [jax.random.randint(jax.random.fold_in(rng, axis), (), 0, length) for axis, length in enumerate(drawn.shape)]
    main_axis = drawn.shape.index(max(drawn.shape))
    neighbour = place[:main_axis] + [(place[main_axis] + 1) % drawn.shape[main_axis]] + place[main_axis + 1:]
    return drawn.at[tuple(place)].set(smallest).at[tuple(neighbour)].set(high)


def block_scale(rng, shape, pieces, least, top_value):
    gain = 1.0
    for position, parts in pieces:
        draws = jax.random.uniform(jax.random.fold_in(jax.random.fold_in(rng, 6), position), (parts,), jnp.float32, least / len(pieces), top_value / len(pieces))
        gain = gain * jnp.repeat(jnp.exp(draws), shape[position] // parts).reshape((-1,) + (1,) * (len(shape) - 1 - position))
    return gain


def bell_draw(key, dims, width, limit, cuts=(), kind=jnp.bfloat16):
    values = width * jax.random.normal(key, dims, jnp.float32)
    if cuts:
        values = values * block_scale(key, dims, cuts, -0.22, 0.18)
    return jnp.clip(values, -limit, limit).astype(kind)


def setup_inputs(seed: int = 0, part: int = 0) -> dict:
    key_list = jax.random.split(jax.random.key(seed), 7)
    own_keys = jax.random.split(jax.random.fold_in(key_list[6], part), 7)
    pre_act = bell_draw(own_keys[0], (EXAMPLES, SEQ, FF), 1.0, 6.0, ((0, 8), (2, 2)))
    out_grad = bell_draw(own_keys[1], (EXAMPLES, SEQ, D), 1.0, 6.0, ((0, 8), (2, 2)))
    counts = with_ends(jax.random.randint(own_keys[2], (EXAMPLES,), 1, SEQ + 1), jax.random.fold_in(own_keys[2], 1), 1, SEQ).astype(jnp.int32)
    proj_in = bell_draw(key_list[3], (FF, RANK), FF ** -0.5, 0.0546875, ((0, 2),))
    proj_out = bell_draw(key_list[4], (D, RANK), D ** -0.5, 0.078125, ((0, 2),))
    query_grads = bell_draw(key_list[5], (QUERIES, RANK * RANK), (RANK * RANK) ** -0.5, 0.09375, ((0, 16),))
    return dict(pre_act=pre_act, out_grad=out_grad, counts=counts, proj_in=proj_in, proj_out=proj_out, query_grads=query_grads)


def reference(pre_act, out_grad, counts, proj_in, proj_out, query_grads):

    def single(items):
        hidden, grad_out, valid = items
        act = jax.nn.gelu(hidden.astype(jnp.float32)).astype(jnp.bfloat16)
        in_proj = jnp.dot(act, proj_in, preferred_element_type=jnp.float32)
        out_proj = jnp.dot(grad_out, proj_out, preferred_element_type=jnp.float32)
        keep = (jnp.arange(SEQ, dtype=jnp.int32) < valid)[:, None]
        out_proj = jnp.where(keep, out_proj, jnp.zeros_like(out_proj))
        grad = jnp.dot(out_proj.T, in_proj, precision=lax.Precision.HIGHEST)
        scale = jnp.sqrt(jnp.mean(grad * grad) + 1e-06)
        return (grad / scale).reshape(-1).astype(jnp.bfloat16)
    flat = lax.map(single, (pre_act, out_grad, counts))
    return lax.dot_general(flat, query_grads, (((1,), (1,)), ((), ())), preferred_element_type=jnp.float32)
```

```python
import functools
import math

import jax
import jax.numpy as jnp
from jax import lax
from jax.experimental import pallas as pl
from jax.experimental.pallas import tpu as pltpu
from jax.sharding import PartitionSpec as P

MESH = pl.DeviceIdType.MESH
NT = (((1,), (1,)), ((), ()))
TN = (((0,), (0,)), ((), ()))
C1 = math.sqrt(2.0 / math.pi)
C2 = C1 * 0.044715


def pieces(size, target):
    step = next(s for s in range(target, 0, -128) if size % s == 0)
    return [(start, step) for start in range(0, size, step)]


def gelu(x):
    x = x.astype(jnp.float32)
    half = 0.5 * x
    return (half + half * jnp.tanh(x * (C1 + C2 * (x * x)))).astype(jnp.bfloat16)


def kernel(
    nd,
    counts,
    pre,
    og,
    wi,
    wo,
    q,
    out,
    x_buf,
    g_buf,
    wi_buf,
    wo_buf,
    q_buf,
    part,
    part_in,
    grad_buf,
    flat,
    rows,
    score,
    score_in,
    x_sem,
    g_sem,
    wi_sem,
    wo_sem,
    q_sem,
    pair_send,
    pair_recv,
    ring_send,
    ring_recv,
):
    group, me, core = lax.axis_index("groups"), lax.axis_index("dp"), lax.axis_index("tensor")
    other = 1 - core
    sibling = (group, me, other)
    rank = wi.shape[0]
    seq, hidden = pre.shape[1:]
    width = og.shape[2]
    nq = q.shape[0]
    x_pieces, g_pieces = pieces(hidden, 768), pieces(width, 1280)
    example = (other, core)

    def x_copy(slot, p):
        start, size = x_pieces[p]
        cols = pl.ds(start, size)
        return pltpu.make_async_copy(pre.at[example[slot], :, cols], x_buf.at[slot, :, cols], x_sem.at[slot, p])

    def g_copy(slot, p):
        start, size = g_pieces[p]
        cols = pl.ds(start, size)
        return pltpu.make_async_copy(og.at[example[slot], :, cols], g_buf.at[slot, :, cols], g_sem.at[slot, p])

    def wi_copy(p):
        start, size = x_pieces[p]
        cols = pl.ds(start, size)
        return pltpu.make_async_copy(wi.at[:, cols], wi_buf.at[:, cols], wi_sem.at[p])

    wo_copy = pltpu.make_async_copy(wo, wo_buf, wo_sem)
    q_copy = pltpu.make_async_copy(q, q_buf.at[pl.ds(0, nq)], q_sem)
    for p in range(len(x_pieces)):
        wi_copy(p).start()
        x_copy(0, p).start()
    wo_copy.start()
    for p in range(len(g_pieces)):
        g_copy(0, p).start()
    q_copy.start()
    for p in range(len(x_pieces)):
        x_copy(1, p).start()
    for p in range(len(g_pieces)):
        g_copy(1, p).start()

    barrier = pltpu.get_barrier_semaphore()
    pl.semaphore_signal(barrier, inc=1, device_id=sibling, device_id_type=MESH)
    for k in range(1, nd):
        pl.semaphore_signal(barrier, inc=1, device_id=(group, lax.rem(me + k, nd), core), device_id_type=MESH)

    def projections(slot):
        total = jnp.zeros((seq, rank), jnp.float32)
        for p, (start, size) in enumerate(x_pieces):
            if slot == 0:
                wi_copy(p).wait()
            x_copy(slot, p).wait()
            for at in range(start, start + size, 256):
                act = gelu(x_buf[slot, :, at : at + 256])
                total += lax.dot_general(act, wi_buf[:, at : at + 256], NT, preferred_element_type=jnp.float32)
        if slot == 0:
            wo_copy.wait()
        outs = jnp.zeros((seq, rank), jnp.float32)
        for p, (start, size) in enumerate(g_pieces):
            g_copy(slot, p).wait()
            outs += lax.dot_general(
                g_buf[slot, :, start : start + size],
                wo_buf[:, start : start + size],
                NT,
                preferred_element_type=jnp.float32,
            )
        return jnp.concatenate([outs, total], axis=1)

    part[...] = projections(0)
    pl.semaphore_wait(barrier, nd)
    part_copy = pltpu.make_async_remote_copy(
        part, part_in, pair_send.at[0], pair_recv.at[0], device_id=sibling, device_id_type=MESH
    )
    part_copy.start()
    q_copy.wait()
    query_copy = pltpu.make_async_remote_copy(
        q_buf.at[pl.ds(0, nq)],
        q_buf.at[pl.ds(nq, nq)],
        pair_send.at[1],
        pair_recv.at[1],
        device_id=sibling,
        device_id_type=MESH,
    )
    query_copy.start()

    own = projections(1)
    part_copy.wait()
    keep = lax.broadcasted_iota(jnp.int32, (seq, 2 * rank), 0) < counts[core]
    joined = jnp.where(keep, own + part_in[...], 0.0)
    gram = lax.dot_general(
        joined, joined, TN, precision=lax.Precision.HIGHEST, preferred_element_type=jnp.float32
    )[:rank]
    upper = lax.broadcasted_iota(jnp.int32, (rank, 2 * rank), 1) >= rank
    grad = jnp.where(upper, gram, pltpu.roll(gram, rank, 1))
    inverse = lax.rsqrt(jnp.sum(grad * grad) / (2 * rank * rank) + 1e-06)
    grad_buf[...] = grad * inverse
    half = rank // 2
    even, odd = grad_buf[pl.ds(0, half, stride=2), :], grad_buf[pl.ds(1, half, stride=2), :]
    flat[me] = jnp.where(upper[:half], odd, even).astype(jnp.bfloat16)

    def ring_copy(k):
        return pltpu.make_async_remote_copy(
            flat.at[me],
            flat.at[me],
            ring_send.at[k],
            ring_recv.at[k],
            device_id=(group, lax.rem(me + k, nd), core),
            device_id_type=MESH,
        )

    for k in range(1, nd):
        ring_copy(k).start()
    query_copy.wait()
    for k in range(1, nd):
        came = flat.at[lax.rem(me + nd - k, nd)]
        pltpu.make_async_remote_copy(
            came,
            came,
            ring_send.at[k],
            ring_recv.at[k],
            device_id=(group, lax.rem(me + k, nd), core),
            device_id_type=MESH,
        ).wait_recv()
    rows[...] = flat[...].astype(jnp.float32).reshape(nd * half, 2 * rank)
    flats = jnp.concatenate([rows[pl.ds(a, nd, stride=half), :] for a in range(half)], axis=1).astype(jnp.bfloat16)
    result = lax.dot_general(flats, q_buf[...], NT, preferred_element_type=jnp.float32)
    score[...] = result
    score_copy = pltpu.make_async_remote_copy(
        score, score_in, pair_send.at[2], pair_recv.at[2], device_id=sibling, device_id_type=MESH
    )
    score_copy.start()
    for k in range(1, nd):
        ring_copy(k).wait_send()
    score_copy.wait()
    mine, theirs = result[:, :nq], score_in[...][:, nq:]
    out[pl.ds(0, nd, stride=2), :] = jnp.where(core == 0, mine, theirs)
    out[pl.ds(1, nd, stride=2), :] = jnp.where(core == 0, theirs, mine)


def shards(nd, pre_act, out_grad, counts, proj_in, proj_out, query_grads):
    examples, seq, hidden = pre_act.shape
    width = out_grad.shape[2]
    rank = proj_in.shape[1]
    nq, flat = query_grads.shape
    assert examples == 2 and flat == rank * rank
    any_space = pl.BlockSpec(memory_space=pltpu.HBM)
    n_x, n_g = len(pieces(hidden, 768)), len(pieces(width, 1280))
    dma = pltpu.SemaphoreType.DMA
    return pl.pallas_call(
        functools.partial(kernel, nd),
        out_shape=jax.ShapeDtypeStruct((nd * examples, nq), jnp.float32),
        in_specs=[pl.BlockSpec(memory_space=pltpu.SMEM)] + [any_space] * 5,
        out_specs=pl.BlockSpec(memory_space=pltpu.VMEM),
        scratch_shapes=[
            pltpu.VMEM((2, seq, hidden), jnp.bfloat16),
            pltpu.VMEM((2, seq, width), jnp.bfloat16),
            pltpu.VMEM((rank, hidden), jnp.bfloat16),
            pltpu.VMEM((rank, width), jnp.bfloat16),
            pltpu.VMEM((2 * nq, flat), jnp.bfloat16),
            pltpu.VMEM((seq, 2 * rank), jnp.float32),
            pltpu.VMEM((seq, 2 * rank), jnp.float32),
            pltpu.VMEM((rank, 2 * rank), jnp.float32),
            pltpu.VMEM((nd, rank // 2, 2 * rank), jnp.bfloat16),
            pltpu.VMEM((nd * rank // 2, 2 * rank), jnp.float32),
            pltpu.VMEM((nd, 2 * nq), jnp.float32),
            pltpu.VMEM((nd, 2 * nq), jnp.float32),
            dma((2, n_x)),
            dma((2, n_g)),
            dma((n_x,)),
            dma,
            dma,
            dma((3,)),
            dma((3,)),
            dma((nd,)),
            dma((nd,)),
        ],
        compiler_params=pltpu.CompilerParams(
            collective_id=0, has_side_effects=True, vmem_limit_bytes=63 * 1024 * 1024
        ),
        cost_estimate=pl.CostEstimate(
            flops=4 * seq * (hidden + width) * rank,
            bytes_accessed=4 * seq * (hidden + width),
            transcendentals=2 * seq * hidden,
        ),
    )(counts, pre_act, out_grad, proj_in.T, proj_out.T, query_grads)


def solution(mesh):
    assert mesh.shape["tensor"] == 2
    return jax.shard_map(
        functools.partial(shards, mesh.shape["dp"]),
        mesh=mesh,
        in_specs=(
            P(("groups", "dp"), None, "tensor"),
            P(("groups", "dp"), None, "tensor"),
            P(("groups", "dp")),
            P("tensor", None),
            P("tensor", None),
            P(("dp", "tensor"), None),
        ),
        out_specs=P("groups", ("dp", "tensor")),
        check_vma=False,
    )
```

```python
import functools
import math

import jax
import jax.numpy as jnp
from jax import lax
from jax.experimental import pallas as pl
from jax.experimental.pallas import tpu as pltpu
from jax.sharding import PartitionSpec as P

MESH = pl.DeviceIdType.MESH
NT = (((1,), (1,)), ((), ()))
TN = (((0,), (0,)), ((), ()))
AHEAD = 8
C1 = math.sqrt(2.0 / math.pi)
C2 = C1 * 0.044715


def pieces(size, target):
    step = next(s for s in range(target, 0, -128) if size % s == 0)
    return [(start, step) for start in range(0, size, step)]


def gelu(x):
    x = x.astype(jnp.float32)
    half = 0.5 * x
    return (half + half * jnp.tanh(x * (C1 + C2 * (x * x)))).astype(jnp.bfloat16)


def kernel(
    nd,
    counts,
    pre,
    og,
    wi,
    wo,
    q,
    out,
    x_buf,
    g_buf,
    wi_buf,
    wo_buf,
    q_buf,
    part,
    part_in,
    grad_buf,
    flat,
    rows,
    score,
    score_in,
    x_sem,
    g_sem,
    wi_sem,
    wo_sem,
    q_sem,
    pair_send,
    pair_recv,
    ring_send,
    ring_recv,
):
    group, me, core = lax.axis_index("groups"), lax.axis_index("dp"), lax.axis_index("tensor")
    other = 1 - core
    sibling = (group, me, other)
    rank = wi.shape[0]
    seq, hidden = pre.shape[1:]
    width = og.shape[2]
    nq = q.shape[0]
    x_pieces, g_pieces = pieces(hidden, 2304), pieces(width, 1280)
    example = (other, core)

    def x_copy(slot, p):
        start, size = x_pieces[p]
        cols = pl.ds(start, size)
        return pltpu.make_async_copy(pre.at[example[slot], :, cols], x_buf.at[slot, :, cols], x_sem.at[slot, p])

    def g_copy(slot, p):
        start, size = g_pieces[p]
        cols = pl.ds(start, size)
        return pltpu.make_async_copy(og.at[example[slot], :, cols], g_buf.at[slot, :, cols], g_sem.at[slot, p])

    def wi_copy(p):
        start, size = x_pieces[p]
        cols = pl.ds(start, size)
        return pltpu.make_async_copy(wi.at[:, cols], wi_buf.at[:, cols], wi_sem.at[p])

    loads = {}
    for p in range(len(x_pieces)):
        loads["wi", p] = wi_copy(p)
        loads["x0", p] = x_copy(0, p)
    loads["wo"] = pltpu.make_async_copy(wo, wo_buf, wo_sem)
    for p in range(len(g_pieces)):
        loads["g0", p] = g_copy(0, p)
    loads["q"] = pltpu.make_async_copy(q, q_buf.at[pl.ds(0, nq)], q_sem)
    for p in range(len(x_pieces)):
        loads["x1", p] = x_copy(1, p)
    for p in range(len(g_pieces)):
        loads["g1", p] = g_copy(1, p)
    queue = list(loads.values())

    def ready(*name):
        loads[name if len(name) > 1 else name[0]].wait()
        if queue:
            queue.pop(0).start()

    for _ in range(AHEAD):
        queue.pop(0).start()

    barrier = pltpu.get_barrier_semaphore()
    pl.semaphore_signal(barrier, inc=1, device_id=sibling, device_id_type=MESH)
    for k in range(1, nd):
        pl.semaphore_signal(barrier, inc=1, device_id=(group, lax.rem(me + k, nd), core), device_id_type=MESH)

    def projections(slot):
        total = jnp.zeros((seq, rank), jnp.float32)
        for p, (start, size) in enumerate(x_pieces):
            if slot == 0:
                ready("wi", p)
            ready(f"x{slot}", p)
            for at in range(start, start + size, 256):
                act = gelu(x_buf[slot, :, at : at + 256])
                total += lax.dot_general(act, wi_buf[:, at : at + 256], NT, preferred_element_type=jnp.float32)
        if slot == 0:
            ready("wo")
        outs = jnp.zeros((seq, rank), jnp.float32)
        for p, (start, size) in enumerate(g_pieces):
            ready(f"g{slot}", p)
            outs += lax.dot_general(
                g_buf[slot, :, start : start + size],
                wo_buf[:, start : start + size],
                NT,
                preferred_element_type=jnp.float32,
            )
        return jnp.concatenate([outs, total], axis=1)

    part[...] = projections(0)
    pl.semaphore_wait(barrier, nd)
    part_copy = pltpu.make_async_remote_copy(
        part, part_in, pair_send.at[0], pair_recv.at[0], device_id=sibling, device_id_type=MESH
    )
    part_copy.start()
    ready("q")
    query_copy = pltpu.make_async_remote_copy(
        q_buf.at[pl.ds(0, nq)],
        q_buf.at[pl.ds(nq, nq)],
        pair_send.at[1],
        pair_recv.at[1],
        device_id=sibling,
        device_id_type=MESH,
    )
    query_copy.start()

    own = projections(1)
    part_copy.wait()
    keep = lax.broadcasted_iota(jnp.int32, (seq, 2 * rank), 0) < counts[core]
    joined = jnp.where(keep, own + part_in[...], 0.0)
    gram = lax.dot_general(
        joined, joined, TN, precision=lax.Precision.HIGHEST, preferred_element_type=jnp.float32
    )[:rank]
    upper = lax.broadcasted_iota(jnp.int32, (rank, 2 * rank), 1) >= rank
    grad = jnp.where(upper, gram, pltpu.roll(gram, rank, 1))
    inverse = lax.rsqrt(jnp.sum(grad * grad) / (2 * rank * rank) + 1e-06)
    grad_buf[...] = grad * inverse
    half = rank // 2
    even, odd = grad_buf[pl.ds(0, half, stride=2), :], grad_buf[pl.ds(1, half, stride=2), :]
    flat[me] = jnp.where(upper[:half], odd, even).astype(jnp.bfloat16)

    def ring_copy(k):
        return pltpu.make_async_remote_copy(
            flat.at[me],
            flat.at[me],
            ring_send.at[k],
            ring_recv.at[k],
            device_id=(group, lax.rem(me + k, nd), core),
            device_id_type=MESH,
        )

    for k in range(1, nd):
        ring_copy(k).start()
    query_copy.wait()
    for k in range(1, nd):
        came = flat.at[lax.rem(me + nd - k, nd)]
        pltpu.make_async_remote_copy(
            came,
            came,
            ring_send.at[k],
            ring_recv.at[k],
            device_id=(group, lax.rem(me + k, nd), core),
            device_id_type=MESH,
        ).wait_recv()
    rows[...] = flat[...].astype(jnp.float32).reshape(nd * half, 2 * rank)
    flats = jnp.concatenate([rows[pl.ds(a, nd, stride=half), :] for a in range(half)], axis=1).astype(jnp.bfloat16)
    score[...] = lax.dot_general(flats, q_buf[nq:, :], NT, preferred_element_type=jnp.float32)
    score_copy = pltpu.make_async_remote_copy(
        score, score_in, pair_send.at[2], pair_recv.at[2], device_id=sibling, device_id_type=MESH
    )
    score_copy.start()
    mine = lax.dot_general(flats, q_buf[:nq, :], NT, preferred_element_type=jnp.float32)
    for k in range(1, nd):
        ring_copy(k).wait_send()
    score_copy.wait()
    theirs = score_in[...]
    out[pl.ds(0, nd, stride=2), :] = jnp.where(core == 0, mine, theirs)
    out[pl.ds(1, nd, stride=2), :] = jnp.where(core == 0, theirs, mine)


def shards(nd, pre_act, out_grad, counts, proj_in, proj_out, query_grads):
    examples, seq, hidden = pre_act.shape
    width = out_grad.shape[2]
    rank = proj_in.shape[1]
    nq, flat = query_grads.shape
    assert examples == 2 and flat == rank * rank
    any_space = pl.BlockSpec(memory_space=pltpu.HBM)
    n_x, n_g = len(pieces(hidden, 2304)), len(pieces(width, 1280))
    dma = pltpu.SemaphoreType.DMA
    return pl.pallas_call(
        functools.partial(kernel, nd),
        out_shape=jax.ShapeDtypeStruct((nd * examples, nq), jnp.float32),
        in_specs=[pl.BlockSpec(memory_space=pltpu.SMEM)] + [any_space] * 5,
        out_specs=pl.BlockSpec(memory_space=pltpu.VMEM),
        scratch_shapes=[
            pltpu.VMEM((2, seq, hidden), jnp.bfloat16),
            pltpu.VMEM((2, seq, width), jnp.bfloat16),
            pltpu.VMEM((rank, hidden), jnp.bfloat16),
            pltpu.VMEM((rank, width), jnp.bfloat16),
            pltpu.VMEM((2 * nq, flat), jnp.bfloat16),
            pltpu.VMEM((seq, 2 * rank), jnp.float32),
            pltpu.VMEM((seq, 2 * rank), jnp.float32),
            pltpu.VMEM((rank, 2 * rank), jnp.float32),
            pltpu.VMEM((nd, rank // 2, 2 * rank), jnp.bfloat16),
            pltpu.VMEM((nd * rank // 2, 2 * rank), jnp.float32),
            pltpu.VMEM((nd, nq), jnp.float32),
            pltpu.VMEM((nd, nq), jnp.float32),
            dma((2, n_x)),
            dma((2, n_g)),
            dma((n_x,)),
            dma,
            dma,
            dma((3,)),
            dma((3,)),
            dma((nd,)),
            dma((nd,)),
        ],
        compiler_params=pltpu.CompilerParams(
            collective_id=0, has_side_effects=True, vmem_limit_bytes=63 * 1024 * 1024
        ),
        cost_estimate=pl.CostEstimate(
            flops=4 * seq * (hidden + width) * rank,
            bytes_accessed=4 * seq * (hidden + width),
            transcendentals=2 * seq * hidden,
        ),
    )(counts, pre_act, out_grad, proj_in.T, proj_out.T, query_grads)


def solution(mesh):
    assert mesh.shape["tensor"] == 2
    return jax.shard_map(
        functools.partial(shards, mesh.shape["dp"]),
        mesh=mesh,
        in_specs=(
            P(("groups", "dp"), None, "tensor"),
            P(("groups", "dp"), None, "tensor"),
            P(("groups", "dp")),
            P("tensor", None),
            P("tensor", None),
            P(("dp", "tensor"), None),
        ),
        out_specs=P("groups", ("dp", "tensor")),
        check_vma=False,
    )
```

```python
import functools
import math

import jax
import jax.numpy as jnp
from jax import lax
from jax.experimental import pallas as pl
from jax.experimental.pallas import tpu as pltpu
from jax.sharding import PartitionSpec as P

MESH = pl.DeviceIdType.MESH
NT = (((1,), (1,)), ((), ()))
TN = (((0,), (0,)), ((), ()))
AHEAD = 8
C1 = math.sqrt(2.0 / math.pi)
C2 = C1 * 0.044715


def pieces(size, target):
    step = next(s for s in range(target, 0, -128) if size % s == 0)
    return [(start, step) for start in range(0, size, step)]


def ramp(size):
    units = pieces(size, 768)
    step, n = units[0][1], len(units)
    cuts = sorted({min(c, n) for c in (1, 5)} | {0, n})
    return [(step * a, step * (b - a)) for a, b in zip(cuts, cuts[1:])]


def gelu(x):
    x = x.astype(jnp.float32)
    half = 0.5 * x
    return (half + half * jnp.tanh(x * (C1 + C2 * (x * x)))).astype(jnp.bfloat16)


def kernel(
    nd,
    counts,
    pre,
    og,
    wi,
    wo,
    q,
    out,
    x_buf,
    g_buf,
    wi_buf,
    wo_buf,
    q_buf,
    part,
    part_in,
    grad_buf,
    flat,
    rows,
    score,
    score_in,
    x_sem,
    g_sem,
    wi_sem,
    wo_sem,
    q_sem,
    pair_send,
    pair_recv,
    ring_send,
    ring_recv,
):
    group, me, core = lax.axis_index("groups"), lax.axis_index("dp"), lax.axis_index("tensor")
    other = 1 - core
    sibling = (group, me, other)
    rank = wi.shape[0]
    seq, hidden = pre.shape[1:]
    width = og.shape[2]
    nq = q.shape[0]
    x_pieces, g_pieces = ramp(hidden), pieces(width, 1280)
    example = (other, core)

    def x_copy(slot, p):
        start, size = x_pieces[p]
        cols = pl.ds(start, size)
        return pltpu.make_async_copy(pre.at[example[slot], :, cols], x_buf.at[slot, :, cols], x_sem.at[slot, p])

    def g_copy(slot, p):
        start, size = g_pieces[p]
        cols = pl.ds(start, size)
        return pltpu.make_async_copy(og.at[example[slot], :, cols], g_buf.at[slot, :, cols], g_sem.at[slot, p])

    def wi_copy(p):
        start, size = x_pieces[p]
        cols = pl.ds(start, size)
        return pltpu.make_async_copy(wi.at[:, cols], wi_buf.at[:, cols], wi_sem.at[p])

    loads = {}
    for p in range(len(x_pieces)):
        loads["wi", p] = wi_copy(p)
        loads["x0", p] = x_copy(0, p)
    loads["wo"] = pltpu.make_async_copy(wo, wo_buf, wo_sem)
    for p in range(len(g_pieces)):
        loads["g0", p] = g_copy(0, p)
    loads["q"] = pltpu.make_async_copy(q, q_buf.at[pl.ds(0, nq)], q_sem)
    for p in range(len(x_pieces)):
        loads["x1", p] = x_copy(1, p)
    for p in range(len(g_pieces)):
        loads["g1", p] = g_copy(1, p)
    queue = list(loads.values())

    def ready(*name):
        loads[name if len(name) > 1 else name[0]].wait()
        if queue:
            queue.pop(0).start()

    for _ in range(AHEAD):
        queue.pop(0).start()

    barrier = pltpu.get_barrier_semaphore()
    pl.semaphore_signal(barrier, inc=1, device_id=sibling, device_id_type=MESH)
    for k in range(1, nd):
        pl.semaphore_signal(barrier, inc=1, device_id=(group, lax.rem(me + k, nd), core), device_id_type=MESH)

    def projections(slot):
        total = jnp.zeros((seq, rank), jnp.float32)
        for p, (start, size) in enumerate(x_pieces):
            if slot == 0:
                ready("wi", p)
            ready(f"x{slot}", p)
            for at in range(start, start + size, 256):
                act = gelu(x_buf[slot, :, at : at + 256])
                total += lax.dot_general(act, wi_buf[:, at : at + 256], NT, preferred_element_type=jnp.float32)
        if slot == 0:
            ready("wo")
        outs = jnp.zeros((seq, rank), jnp.float32)
        for p, (start, size) in enumerate(g_pieces):
            ready(f"g{slot}", p)
            outs += lax.dot_general(
                g_buf[slot, :, start : start + size],
                wo_buf[:, start : start + size],
                NT,
                preferred_element_type=jnp.float32,
            )
        return jnp.concatenate([outs, total], axis=1)

    part[...] = projections(0)
    pl.semaphore_wait(barrier, nd)
    part_copy = pltpu.make_async_remote_copy(
        part, part_in, pair_send.at[0], pair_recv.at[0], device_id=sibling, device_id_type=MESH
    )
    part_copy.start()
    ready("q")
    query_copy = pltpu.make_async_remote_copy(
        q_buf.at[pl.ds(0, nq)],
        q_buf.at[pl.ds(nq, nq)],
        pair_send.at[1],
        pair_recv.at[1],
        device_id=sibling,
        device_id_type=MESH,
    )
    query_copy.start()

    own = projections(1)
    part_copy.wait()
    keep = lax.broadcasted_iota(jnp.int32, (seq, 2 * rank), 0) < counts[core]
    joined = jnp.where(keep, own + part_in[...], 0.0)
    gram = lax.dot_general(
        joined, joined, TN, precision=lax.Precision.HIGHEST, preferred_element_type=jnp.float32
    )[:rank]
    upper = lax.broadcasted_iota(jnp.int32, (rank, 2 * rank), 1) >= rank
    grad = jnp.where(upper, gram, pltpu.roll(gram, rank, 1))
    inverse = lax.rsqrt(jnp.sum(grad * grad) / (2 * rank * rank) + 1e-06)
    grad_buf[...] = grad * inverse
    half = rank // 2
    even, odd = grad_buf[pl.ds(0, half, stride=2), :], grad_buf[pl.ds(1, half, stride=2), :]
    flat[me] = jnp.where(upper[:half], odd, even).astype(jnp.bfloat16)

    def ring_copy(k):
        return pltpu.make_async_remote_copy(
            flat.at[me],
            flat.at[me],
            ring_send.at[k],
            ring_recv.at[k],
            device_id=(group, lax.rem(me + k, nd), core),
            device_id_type=MESH,
        )

    for k in range(1, nd):
        ring_copy(k).start()
    query_copy.wait()
    for k in range(1, nd):
        came = flat.at[lax.rem(me + nd - k, nd)]
        pltpu.make_async_remote_copy(
            came,
            came,
            ring_send.at[k],
            ring_recv.at[k],
            device_id=(group, lax.rem(me + k, nd), core),
            device_id_type=MESH,
        ).wait_recv()
    rows[...] = flat[...].astype(jnp.float32).reshape(nd * half, 2 * rank)
    flats = jnp.concatenate([rows[pl.ds(a, nd, stride=half), :] for a in range(half)], axis=1).astype(jnp.bfloat16)
    score[...] = lax.dot_general(flats, q_buf[nq:, :], NT, preferred_element_type=jnp.float32)
    score_copy = pltpu.make_async_remote_copy(
        score, score_in, pair_send.at[2], pair_recv.at[2], device_id=sibling, device_id_type=MESH
    )
    score_copy.start()
    mine = lax.dot_general(flats, q_buf[:nq, :], NT, preferred_element_type=jnp.float32)
    for k in range(1, nd):
        ring_copy(k).wait_send()
    score_copy.wait()
    theirs = score_in[...]
    out[pl.ds(0, nd, stride=2), :] = jnp.where(core == 0, mine, theirs)
    out[pl.ds(1, nd, stride=2), :] = jnp.where(core == 0, theirs, mine)


def shards(nd, pre_act, out_grad, counts, proj_in, proj_out, query_grads):
    examples, seq, hidden = pre_act.shape
    width = out_grad.shape[2]
    rank = proj_in.shape[1]
    nq, flat = query_grads.shape
    assert examples == 2 and flat == rank * rank
    any_space = pl.BlockSpec(memory_space=pltpu.HBM)
    n_x, n_g = len(ramp(hidden)), len(pieces(width, 1280))
    dma = pltpu.SemaphoreType.DMA
    return pl.pallas_call(
        functools.partial(kernel, nd),
        out_shape=jax.ShapeDtypeStruct((nd * examples, nq), jnp.float32),
        in_specs=[pl.BlockSpec(memory_space=pltpu.SMEM)] + [any_space] * 5,
        out_specs=pl.BlockSpec(memory_space=pltpu.VMEM),
        scratch_shapes=[
            pltpu.VMEM((2, seq, hidden), jnp.bfloat16),
            pltpu.VMEM((2, seq, width), jnp.bfloat16),
            pltpu.VMEM((rank, hidden), jnp.bfloat16),
            pltpu.VMEM((rank, width), jnp.bfloat16),
            pltpu.VMEM((2 * nq, flat), jnp.bfloat16),
            pltpu.VMEM((seq, 2 * rank), jnp.float32),
            pltpu.VMEM((seq, 2 * rank), jnp.float32),
            pltpu.VMEM((rank, 2 * rank), jnp.float32),
            pltpu.VMEM((nd, rank // 2, 2 * rank), jnp.bfloat16),
            pltpu.VMEM((nd * rank // 2, 2 * rank), jnp.float32),
            pltpu.VMEM((nd, nq), jnp.float32),
            pltpu.VMEM((nd, nq), jnp.float32),
            dma((2, n_x)),
            dma((2, n_g)),
            dma((n_x,)),
            dma,
            dma,
            dma((3,)),
            dma((3,)),
            dma((nd,)),
            dma((nd,)),
        ],
        compiler_params=pltpu.CompilerParams(
            collective_id=0, has_side_effects=True, vmem_limit_bytes=63 * 1024 * 1024
        ),
        cost_estimate=pl.CostEstimate(
            flops=4 * seq * (hidden + width) * rank,
            bytes_accessed=4 * seq * (hidden + width),
            transcendentals=2 * seq * hidden,
        ),
    )(counts, pre_act, out_grad, proj_in.T, proj_out.T, query_grads)


def solution(mesh):
    assert mesh.shape["tensor"] == 2
    return jax.shard_map(
        functools.partial(shards, mesh.shape["dp"]),
        mesh=mesh,
        in_specs=(
            P(("groups", "dp"), None, "tensor"),
            P(("groups", "dp"), None, "tensor"),
            P(("groups", "dp")),
            P("tensor", None),
            P("tensor", None),
            P(("dp", "tensor"), None),
        ),
        out_specs=P("groups", ("dp", "tensor")),
        check_vma=False,
    )
```
